1024 devices in a mesh: dp: 32 (over x, z_lo, core), mp: 32 (over y, z_hi).
Axes of the slice: x: 4, y: 8, z: 16 (z_hi: 4, z_lo: 4; z = z_hi * 4 + z_lo), core: 2. Of those that a mesh axis runs over, the one named last changes fastest.
Arguments:
- patches: bfloat16 [32, 256, 6144], P('dp', None, 'mp'), may hold values from -6 to 6
- norm_gain: float32 [6144], replicated, may hold values from 0.1 to 1.9
- w_in: bfloat16 [6144, 24576], P(None, 'mp'), may hold values from -0.076546554 to 0.076546554
- q_gain: float32 [32, 128], P('mp'), may hold values from 0.5 to 9
- k_gain: float32 [32, 128], P('mp'), may hold values from 0.5 to 3
- mlp_bias: float32 [12288], P('mp'), may hold values from -3 to 3
- w_out: bfloat16 [16384, 6144], P('mp', 'dp'), may hold values from -0.046875 to 0.046875
- out_bias: float32 [6144], P('mp'), may hold values from -3 to 3
Outputs:
- mixed: bfloat16 [32, 256, 6144], P('dp', None, 'mp')
The draws below stay inside these ranges and needn't reach their ends.
All inputs are finite; a program needn't handle non-finite values.
Results may differ from the reference program's by a relative error of at most 0.022.
Values may be sent and summed in bfloat16 or wider, within the bound.
No kernel may reach another device: no remote copies, remote signals or barrier semaphores. Data moves between devices by JAX's collectives and lax.ppermute only.
A program may use at most 64 MiB of HBM per device.

```python
import math
import jax
import jax.numpy as jnp
from jax import lax

D = 6144
HEAD_DIM = 128
HEAD_DEV = 1
MLP_DEV = 384
SEQ = 256
HEADS = 32
MLP = 12288
IN_ALL = 24576
HID_ALL = 16384
IMAGES = 32
N_MP = 32


def draw_q_gain(key, part):
    key = jax.random.fold_in(key, 7)
    log_values = jax.random.uniform(key, (HEADS, HEAD_DIM), jnp.float32, math.log(0.5), math.log(3.0))
    gain_values = jnp.exp(log_values)
    return gain_values.astype(jnp.float32)


def draw_k_gain(key, part):
    key = jax.random.fold_in(key, 8)
    log_values = jax.random.uniform(key, (HEADS, HEAD_DIM), jnp.float32, math.log(0.5), math.log(3.0))
    gain_values = jnp.exp(log_values)
    return gain_values.astype(jnp.float32)


def draw_w_in(key, part):
    key = jax.random.fold_in(key, 9)
    base_values = jnp.clip(jax.random.normal(key, (D, IN_ALL), jnp.float32), -4.2, 4.2) / math.sqrt(D)
    weight_values = base_values
    return weight_values.astype(jnp.bfloat16)


def draw_patches(key, part):
    key = jax.random.fold_in(key, 11)
    base_values = jnp.clip(jax.random.normal(key, (IMAGES, SEQ, D), jnp.float32), -6.0, 6.0)
    return base_values.astype(jnp.bfloat16)


def shard_levels(key, shape, pieces, smallest, top_value):
    loudness = 1.0
    for axis_at, parts in pieces:
        draws = jax.random.uniform(jax.random.fold_in(jax.random.fold_in(key, 6), axis_at), (parts,), jnp.float32, smallest / len(pieces), top_value / len(pieces))
        loudness = loudness * jnp.repeat(jnp.exp(draws), shape[axis_at] // parts).reshape((-1,) + (1,) * (len(shape) - 1 - axis_at))
    return loudness


def normal_values(stream_key, shape, scale, reach, pieces=(), kind=jnp.bfloat16):
    factor_of = shard_levels(stream_key, shape, pieces, -0.22, 0.18) if pieces else 1.0
    entries = jax.random.normal(stream_key, shape, jnp.float32) * scale * factor_of
    return jnp.minimum(jnp.maximum(entries, -reach), reach).astype(kind)


def setup_inputs(seed: int = 0) -> dict:
    key_list = jax.random.split(jax.random.key(seed), 9)
    patches = draw_patches(jax.random.fold_in(key_list[8], 71), 0)
    norm_gain = jnp.clip(1.0 + 0.18 * jax.random.normal(key_list[1], (D,), jnp.float32), 0.1, 1.9)
    w_in = draw_w_in(jax.random.fold_in(key_list[8], 71), 0)
    q_gain = draw_q_gain(jax.random.fold_in(key_list[8], 71), 0)
    k_gain = draw_k_gain(jax.random.fold_in(key_list[8], 71), 0)
    mlp_bias = normal_values(key_list[5], (MLP,), 0.5, 3.0, ((0, 32),), jnp.float32)
    w_out = normal_values(key_list[6], (HID_ALL, D), HID_ALL ** -0.5, 0.046875, ((0, 32), (1, 32)))
    out_bias = normal_values(key_list[7], (D,), 0.5, 3.0, ((0, 32),), jnp.float32)
    return {"patches": patches, "norm_gain": norm_gain, "w_in": w_in, "q_gain": q_gain, "k_gain": k_gain, "mlp_bias": mlp_bias, "w_out": w_out, "out_bias": out_bias}


EPS = 1e-06

def normalize(values):
    center = values - lax.optimization_barrier(jnp.mean(values, axis=-1, keepdims=True))
    spread = lax.optimization_barrier(jnp.mean(center * center, axis=-1, keepdims=True))
    return center * lax.rsqrt(spread + EPS)

def reference(patches, norm_gain, w_in, q_gain, k_gain, mlp_bias, w_out, out_bias):
    rows_count = IMAGES * SEQ
    wide = patches.reshape(rows_count, D).astype(jnp.float32)
    normed = (normalize(wide) * norm_gain).astype(jnp.bfloat16)
    in_block = w_in.shape[1] // N_MP
    hid_block = w_out.shape[0] // N_MP
    width_att = HEAD_DEV * HEAD_DIM
    scale_factor = 1.0 / HEAD_DIM ** 0.5

    def step(total, group):
        w_block = lax.dynamic_slice_in_dim(w_in, group * in_block, in_block, 1)
        project = jnp.dot(normed, w_block, preferred_element_type=jnp.float32)
        q_block = lax.dynamic_slice_in_dim(q_gain, group * HEAD_DEV, HEAD_DEV, 0)
        k_block = lax.dynamic_slice_in_dim(k_gain, group * HEAD_DEV, HEAD_DEV, 0)
        bias_block = lax.dynamic_slice_in_dim(mlp_bias, group * MLP_DEV, MLP_DEV, 0)
        o_block = lax.dynamic_slice_in_dim(w_out, group * hid_block, hid_block, 0)
        queries = project[:, :width_att].reshape(IMAGES, SEQ, HEAD_DEV, HEAD_DIM)
        keys = project[:, width_att:2 * width_att].reshape(IMAGES, SEQ, HEAD_DEV, HEAD_DIM)
        values = project[:, 2 * width_att:3 * width_att].astype(jnp.bfloat16).reshape(IMAGES, SEQ, HEAD_DEV, HEAD_DIM)
        mlp_pre = project[:, 3 * width_att:]
        qnorm = normalize(queries) * q_block
        knorm = normalize(keys) * k_block
        scores = jnp.einsum('bqhd,bkhd->bhqk', qnorm, knorm) * scale_factor
        probs = jax.nn.softmax(scores, axis=-1).astype(jnp.bfloat16)
        attended = jnp.einsum('bhqk,bkhd->bqhd', probs.astype(jnp.float32), values.astype(jnp.float32)).astype(jnp.bfloat16)
        mlp_hidden = jax.nn.gelu(mlp_pre + bias_block, approximate=False).astype(jnp.bfloat16)
        hidden = jnp.concatenate([attended.reshape(rows_count, width_att), mlp_hidden], axis=1)
        part = jnp.dot(hidden, o_block, preferred_element_type=jnp.float32).astype(jnp.bfloat16)
        part = lax.optimization_barrier(part)
        return (total + part.astype(jnp.float32), None)
    total, _ = lax.scan(step, jnp.zeros((rows_count, D), jnp.float32), jnp.arange(N_MP, dtype=jnp.int32))
    mixed = (wide + total + out_bias).astype(jnp.bfloat16)
    return mixed.reshape(IMAGES, SEQ, D)
```

```python
import jax
import jax.numpy as jnp
from jax import lax
from jax.sharding import Mesh
from jax.sharding import PartitionSpec as P

EPS = 1e-06
NY = 8
NZ = 4


def normalize(values, axis):
    center = values - jnp.mean(values, axis=axis, keepdims=True)
    spread = jnp.mean(center * center, axis=axis, keepdims=True)
    return center * lax.rsqrt(spread + EPS)


def shift(value, axis, count, by):
    return lax.ppermute(value, axis, [(i, (i + by) % count) for i in range(count)])


def gather_y(block):
    y = lax.axis_index("y")
    half = block.shape[0] // 2
    whole = jnp.zeros((NY,) + block.shape, block.dtype)
    put = lambda whole, part, index, row: lax.dynamic_update_slice(
        whole, part[None], (index % NY, row, 0)
    )
    whole = put(whole, block, y, 0)
    up = down = block
    for step in range(1, 4):
        up, down = shift(up, "y", NY, 1), shift(down, "y", NY, -1)
        whole = put(whole, up, y - step + NY, 0)
        whole = put(whole, down, y + step, 0)
    up = shift(up[:half], "y", NY, 1)
    down = shift(down[half:], "y", NY, -1)
    whole = put(whole, up, y + 4, 0)
    whole = put(whole, down, y + 4, half)
    return whole


def per_device(patches, norm_gain, w_in, q_gain, k_gain, mlp_bias, w_out, out_bias):
    images, seq_len, local_width = patches.shape
    mine = patches[0].T
    zgroup = lax.all_gather(mine, "zh", axis=0, tiled=True)
    w_outT = lax.all_gather(w_out.T, ("x", "zl", "c"), axis=0, tiled=True)
    whole = gather_y(zgroup).reshape(-1, seq_len)
    normed = (normalize(whole.astype(jnp.float32), 0) * norm_gain[:, None]).astype(jnp.bfloat16)
    project = lax.dot_general(
        w_in, normed, (((0,), (0,)), ((), ())), preferred_element_type=jnp.float32
    )
    head = q_gain.shape[1]
    queries = normalize(project[:head], 0) * q_gain[0][:, None]
    keys = normalize(project[head : 2 * head], 0) * k_gain[0][:, None]
    values = project[2 * head : 3 * head].astype(jnp.bfloat16)
    scores = lax.dot_general(queries, keys, (((0,), (0,)), ((), ()))) * (1.0 / head**0.5)
    probs = jax.nn.softmax(scores, axis=-1).astype(jnp.bfloat16)
    attended = lax.dot_general(
        values, probs, (((1,), (1,)), ((), ())), preferred_element_type=jnp.float32
    ).astype(jnp.bfloat16)
    mlp_hidden = jax.nn.gelu(project[3 * head :] + mlp_bias[:, None], approximate=False)
    hidden = jnp.concatenate([attended, mlp_hidden.astype(jnp.bfloat16)], axis=0)
    part = jnp.dot(w_outT, hidden, preferred_element_type=jnp.float32).astype(jnp.bfloat16)
    summed = lax.psum_scatter(part, "y", scatter_dimension=0, tiled=True)
    pieces = lax.all_to_all(summed.reshape(NZ, local_width, seq_len), "zh", 0, 0)
    total = jnp.sum(pieces.astype(jnp.float32), axis=0)
    result = mine.astype(jnp.float32) + total + out_bias[:, None]
    return result.astype(jnp.bfloat16).T[None]


def solution(mesh):
    fine = Mesh(mesh.devices.reshape(4, 4, 2, NY, NZ), ("x", "zl", "c", "y", "zh"))
    dp = ("x", "zl", "c")
    mp = ("y", "zh")
    in_specs = (
        P(dp, None, mp),
        P(),
        P(None, mp),
        P(mp, None),
        P(mp, None),
        P(mp),
        P(mp, dp),
        P(mp),
    )
    return jax.shard_map(
        per_device, mesh=fine, in_specs=in_specs, out_specs=P(dp, None, mp), check_vma=False
    )
```

```python
import jax
import jax.numpy as jnp
from jax import lax
from jax.sharding import Mesh
from jax.sharding import PartitionSpec as P

EPS = 1e-06
NX = 4
NY = 8
NZ = 4
AXES = ("x", "zlh", "zll", "c", "y", "zh")
DP = ("x", "zlh", "zll", "c")
MP = ("y", "zh")


def normalize(values, axis):
    center = values - jnp.mean(values, axis=axis, keepdims=True)
    spread = jnp.mean(center * center, axis=axis, keepdims=True)
    return center * lax.rsqrt(spread + EPS)


def shift(value, axis, count, by):
    return lax.ppermute(value, axis, [(i, (i + by) % count) for i in range(count)])


def gather_y(block):
    y = lax.axis_index("y")
    half = block.shape[0] // 2
    whole = jnp.zeros((NY,) + block.shape, block.dtype)
    put = lambda whole, part, index, row: lax.dynamic_update_slice(
        whole, part[None], (index & (NY - 1), row, 0)
    )
    whole = put(whole, block, y, 0)
    up = down = block
    for step in range(1, 4):
        up, down = shift(up, "y", NY, 1), shift(down, "y", NY, -1)
        whole = put(whole, up, y - step + NY, 0)
        whole = put(whole, down, y + step, 0)
    up = shift(up[:half], "y", NY, 1)
    down = shift(down[half:], "y", NY, -1)
    whole = put(whole, up, y + 4, 0)
    whole = put(whole, down, y + 4, half)
    return whole


def gather_out_weights(w_out):
    depth = w_out.shape[0]
    pairs = [
        ((out * 4 + low) * NY + y, (y * 4 + low) * NY + out)
        for out in range(NY)
        for low in range(4)
        for y in range(NY)
    ]
    swapped = lax.ppermute(w_out.T, ("x", "zlh", "zll", "c", "y"), pairs)
    return lax.all_gather(swapped, DP, axis=0, tiled=True).reshape(NY, -1, depth)


def per_device(patches, norm_gain, w_in, q_gain, k_gain, mlp_bias, w_out, out_bias):
    images, seq_len, local_width = patches.shape
    mine = patches[0].T
    w_rows = gather_out_weights(w_out)
    zgroup = lax.all_gather(mine, "zh", axis=0, tiled=True)
    whole = gather_y(zgroup).reshape(-1, seq_len)
    normed = (normalize(whole.astype(jnp.float32), 0) * norm_gain[:, None]).astype(jnp.bfloat16)
    project = lax.dot_general(
        w_in, normed, (((0,), (0,)), ((), ())), preferred_element_type=jnp.float32
    )
    head = q_gain.shape[1]
    queries = normalize(project[:head], 0) * q_gain[0][:, None]
    keys = normalize(project[head : 2 * head], 0) * k_gain[0][:, None]
    values = project[2 * head : 3 * head].astype(jnp.bfloat16)
    scores = lax.dot_general(queries, keys, (((0,), (0,)), ((), ()))) * (1.0 / head**0.5)
    probs = jax.nn.softmax(scores, axis=-1).astype(jnp.bfloat16)
    attended = lax.dot_general(
        values, probs, (((1,), (1,)), ((), ())), preferred_element_type=jnp.float32
    ).astype(jnp.bfloat16)
    mlp_hidden = jax.nn.gelu(project[3 * head :] + mlp_bias[:, None], approximate=False)
    hidden = jnp.concatenate([attended, mlp_hidden.astype(jnp.bfloat16)], axis=0)
    hidden_all = gather_y(hidden)
    part = jnp.zeros((NZ * local_width, seq_len), jnp.float32)
    for i in range(NY):
        part = part + jnp.dot(w_rows[i], hidden_all[i], preferred_element_type=jnp.float32)
    part = part.astype(jnp.bfloat16).reshape(NZ, local_width, seq_len)
    pieces = lax.all_to_all(part, "zh", 0, 0)
    total = jnp.sum(pieces.astype(jnp.float32), axis=0)
    result = mine.astype(jnp.float32) + total + out_bias[:, None]
    return result.astype(jnp.bfloat16).T[None]


def solution(mesh):
    fine = Mesh(mesh.devices.reshape(NX, 2, 2, 2, NY, NZ), AXES)
    in_specs = (
        P(DP, None, MP),
        P(),
        P(None, MP),
        P(MP, None),
        P(MP, None),
        P(MP),
        P(MP, DP),
        P(MP),
    )
    return jax.shard_map(
        per_device, mesh=fine, in_specs=in_specs, out_specs=P(DP, None, MP), check_vma=False
    )
```

```python
import jax
import jax.numpy as jnp
from jax import lax
from jax.experimental import pallas as pl
from jax.experimental.pallas import tpu as pltpu
from jax.sharding import Mesh
from jax.sharding import PartitionSpec as P

EPS = 1e-06
NX = 4
NY = 8
NZ = 4
AXES = ("x", "zlh", "zll", "c", "y", "zh")
DP = ("x", "zlh", "zll", "c")
MP = ("y", "zh")


def normalize(values, axis):
    center = values - jnp.mean(values, axis=axis, keepdims=True)
    spread = jnp.mean(center * center, axis=axis, keepdims=True)
    return center * lax.rsqrt(spread + EPS)


def shift(value, axis, count, by):
    return lax.ppermute(value, axis, [(i, (i + by) % count) for i in range(count)])


def gather_y(block):
    y = lax.axis_index("y")
    half = block.shape[0] // 2
    whole = jnp.zeros((NY,) + block.shape, block.dtype)
    put = lambda whole, part, index, row: lax.dynamic_update_slice(
        whole, part[None], (index & (NY - 1), row, 0)
    )
    whole = put(whole, block, y, 0)
    up = down = block
    for step in range(1, 4):
        up, down = shift(up, "y", NY, 1), shift(down, "y", NY, -1)
        whole = put(whole, up, y - step + NY, 0)
        whole = put(whole, down, y + step, 0)
    up = shift(up[:half], "y", NY, 1)
    down = shift(down[half:], "y", NY, -1)
    whole = put(whole, up, y + 4, 0)
    whole = put(whole, down, y + 4, half)
    return whole


def gather_out_weights(w_out):
    depth = w_out.shape[0]
    pairs = [
        ((out * 4 + low) * NY + y, (y * 4 + low) * NY + out)
        for out in range(NY)
        for low in range(4)
        for y in range(NY)
    ]
    swapped = lax.ppermute(w_out.T, ("x", "zlh", "zll", "c", "y"), pairs)
    return lax.all_gather(swapped, DP, axis=0, tiled=True).reshape(NY, -1, depth)


def multiply_out(weights, hidden):
    count, rows, depth = weights.shape
    columns = hidden.shape[2]

    def kernel(w_ref, h_ref, o_ref, total_ref):
        step = pl.program_id(0)
        product = jnp.dot(w_ref[0], h_ref[0], preferred_element_type=jnp.float32)

        @pl.when(step == 0)
        def _():
            total_ref[...] = product

        @pl.when(step > 0)
        def _():
            total_ref[...] += product

        @pl.when(step == count - 1)
        def _():
            o_ref[...] = total_ref[...].astype(o_ref.dtype)

    return pl.pallas_call(
        kernel,
        grid=(count,),
        in_specs=[
            pl.BlockSpec((1, rows, depth), lambda i: (i, 0, 0)),
            pl.BlockSpec((1, depth, columns), lambda i: (i, 0, 0)),
        ],
        out_specs=pl.BlockSpec((rows, columns), lambda i: (0, 0)),
        out_shape=jax.ShapeDtypeStruct((rows, columns), jnp.bfloat16),
        scratch_shapes=[pltpu.VMEM((rows, columns), jnp.float32)],
        compiler_params=pltpu.CompilerParams(vmem_limit_bytes=56 * 1024 * 1024),
        cost_estimate=pl.CostEstimate(
            flops=2 * count * rows * depth * columns,
            bytes_accessed=2 * count * depth * (rows + columns),
            transcendentals=0,
        ),
    )(weights, hidden)


def per_device(patches, norm_gain, w_in, q_gain, k_gain, mlp_bias, w_out, out_bias):
    images, seq_len, local_width = patches.shape
    mine = patches[0].T
    zgroup = lax.all_gather(mine, "zh", axis=0, tiled=True)
    w_rows = gather_out_weights(w_out + zgroup[0, 0] * 0)
    whole = gather_y(zgroup).reshape(-1, seq_len)
    normed = (normalize(whole.astype(jnp.float32), 0) * norm_gain[:, None]).astype(jnp.bfloat16)
    project = lax.dot_general(
        w_in, normed, (((0,), (0,)), ((), ())), preferred_element_type=jnp.float32
    )
    head = q_gain.shape[1]
    queries = normalize(project[:head], 0) * q_gain[0][:, None]
    keys = normalize(project[head : 2 * head], 0) * k_gain[0][:, None]
    values = project[2 * head : 3 * head].astype(jnp.bfloat16)
    scores = lax.dot_general(queries, keys, (((0,), (0,)), ((), ()))) * (1.0 / head**0.5)
    probs = jax.nn.softmax(scores, axis=-1).astype(jnp.bfloat16)
    attended = lax.dot_general(
        values, probs, (((1,), (1,)), ((), ())), preferred_element_type=jnp.float32
    ).astype(jnp.bfloat16)
    mlp_hidden = jax.nn.gelu(project[3 * head :] + mlp_bias[:, None], approximate=False)
    hidden = jnp.concatenate([attended, mlp_hidden.astype(jnp.bfloat16)], axis=0)
    hidden_all = gather_y(hidden)
    part = multiply_out(w_rows, hidden_all).reshape(NZ, local_width, seq_len)
    pieces = lax.all_to_all(part, "zh", 0, 0)
    total = jnp.sum(pieces.astype(jnp.float32), axis=0)
    result = mine.astype(jnp.float32) + total + out_bias[:, None]
    return result.astype(jnp.bfloat16).T[None]


def solution(mesh):
    fine = Mesh(mesh.devices.reshape(NX, 2, 2, 2, NY, NZ), AXES)
    in_specs = (
        P(DP, None, MP),
        P(),
        P(None, MP),
        P(MP, None),
        P(MP, None),
        P(MP),
        P(MP, DP),
        P(MP),
    )
    return jax.shard_map(
        per_device, mesh=fine, in_specs=in_specs, out_specs=P(DP, None, MP), check_vma=False
    )
```

```python
import jax
import jax.numpy as jnp
from jax import lax
from jax.experimental import pallas as pl
from jax.experimental.pallas import tpu as pltpu
from jax.sharding import Mesh
from jax.sharding import PartitionSpec as P

EPS = 1e-06
NX = 4
NY = 8
NZ = 4
AXES = ("x", "zlh", "zll", "c", "y", "zh")
DP = ("x", "zlh", "zll", "c")
MP = ("y", "zh")


def normalize(values, axis):
    center = values - jnp.mean(values, axis=axis, keepdims=True)
    spread = jnp.mean(center * center, axis=axis, keepdims=True)
    return center * lax.rsqrt(spread + EPS)


def shift(value, axis, count, by):
    return lax.ppermute(value, axis, [(i, (i + by) % count) for i in range(count)])


def gather_y(block, early=None):
    y = lax.axis_index("y")
    half = block.shape[0] // 2
    whole = jnp.zeros((NY,) + block.shape, block.dtype)
    put = lambda whole, part, index, row: lax.dynamic_update_slice(
        whole, part[None], (index & (NY - 1), row, 0)
    )
    whole = put(whole, block, y, 0)
    up = down = block
    for step in range(1, 4):
        up, down = shift(up, "y", NY, 1), shift(down, "y", NY, -1)
        whole = put(whole, up, y - step + NY, 0)
        whole = put(whole, down, y + step, 0)
    up, down = shift(up[:half], "y", NY, 1), shift(down[half:], "y", NY, -1)
    if early is not None:
        return early(whole), jnp.concatenate([up, down], axis=0)
    whole = put(whole, up, y + 4, 0)
    return put(whole, down, y + 4, half)


def swap_out_weights(w_out):
    pairs = [
        ((out * 4 + low) * NY + y, (y * 4 + low) * NY + out)
        for out in range(NY)
        for low in range(4)
        for y in range(NY)
    ]
    return lax.ppermute(w_out.T, ("x", "zlh", "zll", "c", "y"), pairs)


def multiply_out(weights, hidden, first, steps):
    count, rows, depth = weights.shape
    columns = hidden.shape[2]

    def kernel(first_ref, w_ref, h_ref, o_ref):
        product = jnp.dot(w_ref[0], h_ref[0], preferred_element_type=jnp.float32)

        @pl.when(pl.program_id(0) == 0)
        def _():
            o_ref[...] = product

        @pl.when(pl.program_id(0) > 0)
        def _():
            o_ref[...] += product

    place = lambda i, first_ref: ((first_ref[0] + i) & (count - 1), 0, 0)
    return pl.pallas_call(
        kernel,
        grid_spec=pltpu.PrefetchScalarGridSpec(
            num_scalar_prefetch=1,
            grid=(steps,),
            in_specs=[
                pl.BlockSpec((1, rows, depth), place),
                pl.BlockSpec((1, depth, columns), place),
            ],
            out_specs=pl.BlockSpec((rows, columns), lambda i, first_ref: (0, 0)),
        ),
        out_shape=jax.ShapeDtypeStruct((rows, columns), jnp.float32),
        compiler_params=pltpu.CompilerParams(vmem_limit_bytes=16 * 1024 * 1024),
        cost_estimate=pl.CostEstimate(
            flops=2 * steps * rows * depth * columns,
            bytes_accessed=2 * steps * depth * (rows + columns) + 4 * rows * columns,
            transcendentals=0,
        ),
    )(first[None], weights, hidden)


def per_device(patches, norm_gain, w_in, q_gain, k_gain, mlp_bias, w_out, out_bias):
    images, seq_len, local_width = patches.shape
    mine = patches[0].T
    swapped = swap_out_weights(w_out)
    zgroup = lax.all_gather(mine, "zh", axis=0, tiled=True)
    w_rows = lax.all_gather(swapped + zgroup[0, 0] * 0, DP, axis=0, tiled=True)
    w_rows = w_rows.reshape(NY, NZ * local_width, -1)
    whole = gather_y(zgroup).reshape(-1, seq_len)
    normed = (normalize(whole.astype(jnp.float32), 0) * norm_gain[:, None]).astype(jnp.bfloat16)
    project = lax.dot_general(
        w_in, normed, (((0,), (0,)), ((), ())), preferred_element_type=jnp.float32
    )
    head = q_gain.shape[1]
    queries = normalize(project[:head], 0) * q_gain[0][:, None]
    keys = normalize(project[head : 2 * head], 0) * k_gain[0][:, None]
    values = project[2 * head : 3 * head].astype(jnp.bfloat16)
    scores = lax.dot_general(queries, keys, (((0,), (0,)), ((), ()))) * (1.0 / head**0.5)
    probs = jax.nn.softmax(scores, axis=-1).astype(jnp.bfloat16)
    attended = lax.dot_general(
        values, probs, (((1,), (1,)), ((), ())), preferred_element_type=jnp.float32
    ).astype(jnp.bfloat16)
    mlp_hidden = jax.nn.gelu(project[3 * head :] + mlp_bias[:, None], approximate=False)
    hidden = jnp.concatenate([attended, mlp_hidden.astype(jnp.bfloat16)], axis=0)
    far = (lax.axis_index("y") + 4) & (NY - 1)
    near_part, far_hidden = gather_y(
        hidden, lambda near: multiply_out(w_rows, near, far + 1, NY - 1)
    )
    far_weights = lax.dynamic_index_in_dim(w_rows, far, 0, False)
    part = near_part + jnp.dot(far_weights, far_hidden, preferred_element_type=jnp.float32)
    part = part.astype(jnp.bfloat16).reshape(NZ, local_width, seq_len)
    pieces = lax.all_to_all(part, "zh", 0, 0)
    total = jnp.sum(pieces.astype(jnp.float32), axis=0)
    result = mine.astype(jnp.float32) + total + out_bias[:, None]
    return result.astype(jnp.bfloat16).T[None]


def solution(mesh):
    fine = Mesh(mesh.devices.reshape(NX, 2, 2, 2, NY, NZ), AXES)
    in_specs = (
        P(DP, None, MP),
        P(),
        P(None, MP),
        P(MP, None),
        P(MP, None),
        P(MP),
        P(MP, DP),
        P(MP),
    )
    return jax.shard_map(
        per_device, mesh=fine, in_specs=in_specs, out_specs=P(DP, None, MP), check_vma=False
    )
```

```python
import jax
import jax.numpy as jnp
from jax import lax
from jax.experimental import pallas as pl
from jax.experimental.pallas import tpu as pltpu
from jax.sharding import Mesh
from jax.sharding import PartitionSpec as P

EPS = 1e-06
NX = 4
NY = 8
NZ = 4
AXES = ("x", "zlh", "zll", "c", "y", "zh")
DP = ("x", "zlh", "zll", "c")
MP = ("y", "zh")


def normalize(values, axis):
    center = values - jnp.mean(values, axis=axis, keepdims=True)
    spread = jnp.mean(center * center, axis=axis, keepdims=True)
    return center * lax.rsqrt(spread + EPS)


def gather_direct(block, axis, count):
    return lax.all_to_all(jnp.broadcast_to(block, (count,) + block.shape), axis, 0, 0)


def swap_out_weights(w_out):
    pairs = [
        ((out * 4 + low) * NY + y, (y * 4 + low) * NY + out)
        for out in range(NY)
        for low in range(4)
        for y in range(NY)
    ]
    return lax.ppermute(w_out.T, ("x", "zlh", "zll", "c", "y"), pairs)


def multiply_out(weights, hidden):
    count, rows, depth = weights.shape
    columns = hidden.shape[2]

    def kernel(w_ref, h_ref, o_ref, total_ref):
        step = pl.program_id(0)
        product = jnp.dot(w_ref[0], h_ref[0], preferred_element_type=jnp.float32)

        @pl.when(step == 0)
        def _():
            total_ref[...] = product

        @pl.when((step > 0) & (step < count - 1))
        def _():
            total_ref[...] += product

        @pl.when(step == count - 1)
        def _():
            o_ref[...] = (total_ref[...] + product).astype(o_ref.dtype)

    return pl.pallas_call(
        kernel,
        grid=(count,),
        in_specs=[
            pl.BlockSpec((1, rows, depth), lambda i: (i, 0, 0)),
            pl.BlockSpec((1, depth, columns), lambda i: (i, 0, 0)),
        ],
        out_specs=pl.BlockSpec((rows, columns), lambda i: (0, 0)),
        out_shape=jax.ShapeDtypeStruct((rows, columns), jnp.bfloat16),
        scratch_shapes=[pltpu.VMEM((rows, columns), jnp.float32)],
        compiler_params=pltpu.CompilerParams(vmem_limit_bytes=16 * 1024 * 1024),
        cost_estimate=pl.CostEstimate(
            flops=2 * count * rows * depth * columns,
            bytes_accessed=2 * count * depth * (rows + columns),
            transcendentals=0,
        ),
    )(weights, hidden)


def per_device(patches, norm_gain, w_in, q_gain, k_gain, mlp_bias, w_out, out_bias):
    images, seq_len, local_width = patches.shape
    mine = patches[0].T
    swapped = swap_out_weights(w_out)
    zgroup = gather_direct(mine, "zh", NZ).reshape(NZ * local_width, seq_len)
    w_rows = lax.all_gather(swapped + zgroup[0, 0] * 0, DP, axis=0, tiled=True)
    w_rows = w_rows.reshape(NY, NZ * local_width, -1)
    whole = gather_direct(zgroup, "y", NY).reshape(-1, seq_len)
    normed = (normalize(whole.astype(jnp.float32), 0) * norm_gain[:, None]).astype(jnp.bfloat16)
    project = lax.dot_general(
        w_in, normed, (((0,), (0,)), ((), ())), preferred_element_type=jnp.float32
    )
    head = q_gain.shape[1]
    queries = normalize(project[:head], 0) * q_gain[0][:, None]
    keys = normalize(project[head : 2 * head], 0) * k_gain[0][:, None]
    values = project[2 * head : 3 * head].astype(jnp.bfloat16)
    scores = lax.dot_general(queries, keys, (((0,), (0,)), ((), ()))) * (1.0 / head**0.5)
    probs = jax.nn.softmax(scores, axis=-1).astype(jnp.bfloat16)
    attended = lax.dot_general(
        values, probs, (((1,), (1,)), ((), ())), preferred_element_type=jnp.float32
    ).astype(jnp.bfloat16)
    mlp_hidden = jax.nn.gelu(project[3 * head :] + mlp_bias[:, None], approximate=False)
    hidden = jnp.concatenate([attended, mlp_hidden.astype(jnp.bfloat16)], axis=0)
    part = multiply_out(w_rows, gather_direct(hidden, "y", NY))
    part = part.reshape(NZ, local_width, seq_len)
    pieces = lax.all_to_all(part, "zh", 0, 0)
    total = jnp.sum(pieces.astype(jnp.float32), axis=0)
    result = mine.astype(jnp.float32) + total + out_bias[:, None]
    return result.astype(jnp.bfloat16).T[None]


def solution(mesh):
    fine = Mesh(mesh.devices.reshape(NX, 2, 2, 2, NY, NZ), AXES)
    in_specs = (
        P(DP, None, MP),
        P(),
        P(None, MP),
        P(MP, None),
        P(MP, None),
        P(MP),
        P(MP, DP),
        P(MP),
    )
    return jax.shard_map(
        per_device, mesh=fine, in_specs=in_specs, out_specs=P(DP, None, MP), check_vma=False
    )
```

```python
import jax
import jax.numpy as jnp
from jax import lax
from jax.experimental import pallas as pl
from jax.experimental.pallas import tpu as pltpu
from jax.sharding import Mesh
from jax.sharding import PartitionSpec as P

EPS = 1e-06
NX = 4
NY = 8
NZ = 4
AXES = ("x", "zlh", "zll", "c", "y", "zh")
DP = ("x", "zlh", "zll", "c")
MP = ("y", "zh")


def normalize(values, axis):
    center = values - jnp.mean(values, axis=axis, keepdims=True)
    spread = jnp.mean(center * center, axis=axis, keepdims=True)
    return center * lax.rsqrt(spread + EPS)


def shift(value, axis, count, by):
    return lax.ppermute(value, axis, [(i, (i + by) % count) for i in range(count)])


def gather_y(block):
    half = block.shape[0] // 2
    below2, above2 = shift(block, "y", NY, 2), shift(block, "y", NY, -2)
    below1, above1 = shift(block, "y", NY, 1), shift(block, "y", NY, -1)
    below3, above3 = shift(below2, "y", NY, 1), shift(above2, "y", NY, -1)
    far_top = shift(below2[:half], "y", NY, 2)
    far_bottom = shift(above2[half:], "y", NY, -2)
    return (below2, below1, block, above1, above2), (above3, far_top, far_bottom, below3)


def gather_in_order(block):
    y = lax.axis_index("y")
    half = block.shape[0] // 2
    near, (above3, far_top, far_bottom, below3) = gather_y(block)
    whole = jnp.zeros((NY,) + block.shape, block.dtype)
    put = lambda whole, part, index, row: lax.dynamic_update_slice(
        whole, part[None], (index & (NY - 1), row, 0)
    )
    for i, part in enumerate(near):
        whole = put(whole, part, y + NY - 2 + i, 0)
    whole = put(whole, above3, y + 3, 0)
    whole = put(whole, below3, y + 5, 0)
    whole = put(whole, far_top, y + 4, 0)
    return put(whole, far_bottom, y + 4, half)


def swap_out_weights(w_out):
    pairs = [
        ((out * 4 + low) * NY + y, (y * 4 + low) * NY + out)
        for out in range(NY)
        for low in range(4)
        for y in range(NY)
    ]
    return lax.ppermute(w_out.T, ("x", "zlh", "zll", "c", "y"), pairs)


def multiply_out(weights, hidden, first):
    count, rows, depth = weights.shape
    columns = hidden.shape[2]

    def kernel(first_ref, w_ref, h_ref, o_ref, total_ref):
        step = pl.program_id(0)
        product = jnp.dot(w_ref[0], h_ref[0], preferred_element_type=jnp.float32)

        @pl.when(step == 0)
        def _():
            total_ref[...] = product

        @pl.when((step > 0) & (step < count - 1))
        def _():
            total_ref[...] += product

        @pl.when(step == count - 1)
        def _():
            o_ref[...] = (total_ref[...] + product).astype(o_ref.dtype)

    return pl.pallas_call(
        kernel,
        grid_spec=pltpu.PrefetchScalarGridSpec(
            num_scalar_prefetch=1,
            grid=(count,),
            in_specs=[
                pl.BlockSpec(
                    (1, rows, depth), lambda i, first_ref: ((first_ref[0] + i) & (count - 1), 0, 0)
                ),
                pl.BlockSpec((1, depth, columns), lambda i, first_ref: (i, 0, 0)),
            ],
            out_specs=pl.BlockSpec((rows, columns), lambda i, first_ref: (0, 0)),
            scratch_shapes=[pltpu.VMEM((rows, columns), jnp.float32)],
        ),
        out_shape=jax.ShapeDtypeStruct((rows, columns), jnp.bfloat16),
        compiler_params=pltpu.CompilerParams(vmem_limit_bytes=16 * 1024 * 1024),
        cost_estimate=pl.CostEstimate(
            flops=2 * count * rows * depth * columns,
            bytes_accessed=2 * count * depth * (rows + columns),
            transcendentals=0,
        ),
    )(first[None], weights, hidden)


def per_device(patches, norm_gain, w_in, q_gain, k_gain, mlp_bias, w_out, out_bias):
    images, seq_len, local_width = patches.shape
    mine = patches[0].T
    swapped = swap_out_weights(w_out)
    zgroup = lax.all_gather(mine, "zh", axis=0, tiled=True)
    w_rows = lax.all_gather(swapped + zgroup[0, 0] * 0, DP, axis=0, tiled=True)
    w_rows = w_rows.reshape(NY, NZ * local_width, -1)
    whole = gather_in_order(zgroup).reshape(-1, seq_len)
    normed = (normalize(whole.astype(jnp.float32), 0) * norm_gain[:, None]).astype(jnp.bfloat16)
    project = lax.dot_general(
        w_in, normed, (((0,), (0,)), ((), ())), preferred_element_type=jnp.float32
    )
    head = q_gain.shape[1]
    queries = normalize(project[:head], 0) * q_gain[0][:, None]
    keys = normalize(project[head : 2 * head], 0) * k_gain[0][:, None]
    values = project[2 * head : 3 * head].astype(jnp.bfloat16)
    scores = lax.dot_general(queries, keys, (((0,), (0,)), ((), ()))) * (1.0 / head**0.5)
    probs = jax.nn.softmax(scores, axis=-1).astype(jnp.bfloat16)
    attended = lax.dot_general(
        values, probs, (((1,), (1,)), ((), ())), preferred_element_type=jnp.float32
    ).astype(jnp.bfloat16)
    mlp_hidden = jax.nn.gelu(project[3 * head :] + mlp_bias[:, None], approximate=False)
    hidden = jnp.concatenate([attended, mlp_hidden.astype(jnp.bfloat16)], axis=0)
    near, (above3, far_top, far_bottom, below3) = gather_y(hidden)
    far = jnp.concatenate([far_top, far_bottom], axis=0)
    hidden_all = jnp.stack(near + (above3, far, below3))
    part = multiply_out(w_rows, hidden_all, lax.axis_index("y") + NY - 2)
    part = part.reshape(NZ, local_width, seq_len)
    pieces = lax.all_to_all(part, "zh", 0, 0)
    total = jnp.sum(pieces.astype(jnp.float32), axis=0)
    result = mine.astype(jnp.float32) + total + out_bias[:, None]
    return result.astype(jnp.bfloat16).T[None]


def solution(mesh):
    fine = Mesh(mesh.devices.reshape(NX, 2, 2, 2, NY, NZ), AXES)
    in_specs = (
        P(DP, None, MP),
        P(),
        P(None, MP),
        P(MP, None),
        P(MP, None),
        P(MP),
        P(MP, DP),
        P(MP),
    )
    return jax.shard_map(
        per_device, mesh=fine, in_specs=in_specs, out_specs=P(DP, None, MP), check_vma=False
    )
```

```python
import jax
import jax.numpy as jnp
from jax import lax
from jax.experimental import pallas as pl
from jax.experimental.pallas import tpu as pltpu
from jax.sharding import Mesh
from jax.sharding import PartitionSpec as P

EPS = 1e-06
NX = 4
NY = 8
NZ = 4
AXES = ("x", "zlh", "zll", "c", "y", "zh")
DP = ("x", "zlh", "zll", "c")
MP = ("y", "zh")


def normalize(values, axis):
    center = values - jnp.mean(values, axis=axis, keepdims=True)
    spread = jnp.mean(center * center, axis=axis, keepdims=True)
    return center * lax.rsqrt(spread + EPS)


def shift(value, axis, count, by):
    return lax.ppermute(value, axis, [(i, (i + by) % count) for i in range(count)])


def gather_y(block, zero=None):
    half = block.shape[0] // 2
    below2, above2 = shift(block, "y", NY, 2), shift(block, "y", NY, -2)
    below1, above1 = shift(block, "y", NY, 1), shift(block, "y", NY, -1)
    late = above2 if zero is None else above2 + zero
    below3, above3 = shift(below2, "y", NY, 1), shift(late, "y", NY, -1)
    far_top = shift(below2[:half], "y", NY, 2)
    far_bottom = shift(above2[half:], "y", NY, -2)
    return (below2, below1, block, above1, above2), (above3, far_top, far_bottom, below3)


def gather_in_order(block):
    y = lax.axis_index("y")
    half = block.shape[0] // 2
    near, (above3, far_top, far_bottom, below3) = gather_y(block)
    whole = jnp.zeros((NY,) + block.shape, block.dtype)
    put = lambda whole, part, index, row: lax.dynamic_update_slice(
        whole, part[None], (index & (NY - 1), row, 0)
    )
    for i, part in enumerate(near):
        whole = put(whole, part, y + NY - 2 + i, 0)
    whole = put(whole, above3, y + 3, 0)
    whole = put(whole, below3, y + 5, 0)
    whole = put(whole, far_top, y + 4, 0)
    return put(whole, far_bottom, y + 4, half)


def swap_out_weights(w_out):
    pairs = [
        ((out * 4 + low) * NY + y, (y * 4 + low) * NY + out)
        for out in range(NY)
        for low in range(4)
        for y in range(NY)
    ]
    return lax.ppermute(w_out.T, ("x", "zlh", "zll", "c", "y"), pairs)


def multiply_out(weights, hidden, first):
    count, rows, depth = weights.shape
    steps, _, columns = hidden.shape

    def kernel(first_ref, w_ref, h_ref, o_ref):
        product = jnp.dot(w_ref[0], h_ref[0], preferred_element_type=jnp.float32)

        @pl.when(pl.program_id(0) == 0)
        def _():
            o_ref[...] = product

        @pl.when(pl.program_id(0) > 0)
        def _():
            o_ref[...] += product

    return pl.pallas_call(
        kernel,
        grid_spec=pltpu.PrefetchScalarGridSpec(
            num_scalar_prefetch=1,
            grid=(steps,),
            in_specs=[
                pl.BlockSpec(
                    (1, rows, depth), lambda i, first_ref: ((first_ref[0] + i) & (count - 1), 0, 0)
                ),
                pl.BlockSpec((1, depth, columns), lambda i, first_ref: (i, 0, 0)),
            ],
            out_specs=pl.BlockSpec((rows, columns), lambda i, first_ref: (0, 0)),
        ),
        out_shape=jax.ShapeDtypeStruct((rows, columns), jnp.float32),
        compiler_params=pltpu.CompilerParams(vmem_limit_bytes=16 * 1024 * 1024),
        cost_estimate=pl.CostEstimate(
            flops=2 * steps * rows * depth * columns,
            bytes_accessed=2 * steps * depth * (rows + columns) + 4 * rows * columns,
            transcendentals=0,
        ),
    )(first[None], weights, hidden)


def per_device(patches, norm_gain, w_in, q_gain, k_gain, mlp_bias, w_out, out_bias):
    images, seq_len, local_width = patches.shape
    mine = patches[0].T
    swapped = swap_out_weights(w_out)
    zgroup = lax.all_gather(mine, "zh", axis=0, tiled=True)
    w_rows = lax.all_gather(swapped + zgroup[0, 0] * 0, DP, axis=0, tiled=True)
    w_rows = w_rows.reshape(NY, NZ * local_width, -1)
    whole = gather_in_order(zgroup).reshape(-1, seq_len)
    normed = (normalize(whole.astype(jnp.float32), 0) * norm_gain[:, None]).astype(jnp.bfloat16)
    project = lax.dot_general(
        w_in, normed, (((0,), (0,)), ((), ())), preferred_element_type=jnp.float32
    )
    head = q_gain.shape[1]
    queries = normalize(project[:head], 0) * q_gain[0][:, None]
    keys = normalize(project[head : 2 * head], 0) * k_gain[0][:, None]
    values = project[2 * head : 3 * head].astype(jnp.bfloat16)
    scores = lax.dot_general(queries, keys, (((0,), (0,)), ((), ()))) * (1.0 / head**0.5)
    probs = jax.nn.softmax(scores, axis=-1).astype(jnp.bfloat16)
    attended = lax.dot_general(
        values, probs, (((1,), (1,)), ((), ())), preferred_element_type=jnp.float32
    ).astype(jnp.bfloat16)
    mlp_hidden = jax.nn.gelu(project[3 * head :] + mlp_bias[:, None], approximate=False)
    hidden = jnp.concatenate([attended, mlp_hidden.astype(jnp.bfloat16)], axis=0)
    near, (above3, far_top, far_bottom, below3) = gather_y(hidden, w_rows[0, 0, 0] * 0)
    far = jnp.concatenate([far_top, far_bottom], axis=0)
    y = lax.axis_index("y")
    part = multiply_out(w_rows, jnp.stack(near), y + NY - 2)
    part = part + multiply_out(w_rows, jnp.stack((above3, far, below3)), y + 3)
    part = part.astype(jnp.bfloat16).reshape(NZ, local_width, seq_len)
    pieces = lax.all_to_all(part, "zh", 0, 0)
    total = jnp.sum(pieces.astype(jnp.float32), axis=0)
    result = mine.astype(jnp.float32) + total + out_bias[:, None]
    return result.astype(jnp.bfloat16).T[None]


def solution(mesh):
    fine = Mesh(mesh.devices.reshape(NX, 2, 2, 2, NY, NZ), AXES)
    in_specs = (
        P(DP, None, MP),
        P(),
        P(None, MP),
        P(MP, None),
        P(MP, None),
        P(MP),
        P(MP, DP),
        P(MP),
    )
    return jax.shard_map(
        per_device, mesh=fine, in_specs=in_specs, out_specs=P(DP, None, MP), check_vma=False
    )
```

```python
import jax
import jax.numpy as jnp
from jax import lax
from jax.experimental import pallas as pl
from jax.experimental.pallas import tpu as pltpu
from jax.sharding import Mesh
from jax.sharding import PartitionSpec as P

EPS = 1e-06
NX = 4
NY = 8
NZ = 4
AXES = ("x", "zlh", "zll", "c", "y", "zh")
DP = ("x", "zlh", "zll", "c")
MP = ("y", "zh")


def normalize(values, axis):
    center = values - jnp.mean(values, axis=axis, keepdims=True)
    spread = jnp.mean(center * center, axis=axis, keepdims=True)
    return center * lax.rsqrt(spread + EPS)


def shift(value, axis, count, by):
    return lax.ppermute(value, axis, [(i, (i + by) % count) for i in range(count)])


def gather_y(block, zero=None):
    half = block.shape[0] // 2
    below2, above2 = shift(block, "y", NY, 2), shift(block, "y", NY, -2)
    below1, above1 = shift(block, "y", NY, 1), shift(block, "y", NY, -1)
    late = above2 if zero is None else above2 + zero
    below3, above3 = shift(below2, "y", NY, 1), shift(late, "y", NY, -1)
    far_top = shift(below2[:half], "y", NY, 2)
    far_bottom = shift(above2[half:], "y", NY, -2)
    return (below2, below1, block, above1, above2), (above3, far_top, far_bottom, below3)


def gather_in_order(block):
    y = lax.axis_index("y")
    half = block.shape[0] // 2
    near, (above3, far_top, far_bottom, below3) = gather_y(block)
    whole = jnp.zeros((NY,) + block.shape, block.dtype)
    put = lambda whole, part, index, row: lax.dynamic_update_slice(
        whole, part[None], (index & (NY - 1), row, 0)
    )
    for i, part in enumerate(near):
        whole = put(whole, part, y + NY - 2 + i, 0)
    whole = put(whole, above3, y + 3, 0)
    whole = put(whole, below3, y + 5, 0)
    whole = put(whole, far_top, y + 4, 0)
    return put(whole, far_bottom, y + 4, half)


def swap_out_weights(w_out):
    pairs = [
        ((out * 4 + low) * NY + y, (y * 4 + low) * NY + out)
        for out in range(NY)
        for low in range(4)
        for y in range(NY)
    ]
    return lax.ppermute(w_out.T, ("x", "zlh", "zll", "c", "y"), pairs)


def multiply_out(weights, hidden, first):
    count, rows, depth = weights.shape
    steps, _, columns = hidden.shape

    def kernel(first_ref, w_ref, h_ref, o_ref):
        product = jnp.dot(w_ref[0], h_ref[0], preferred_element_type=jnp.float32)

        @pl.when(pl.program_id(0) == 0)
        def _():
            o_ref[...] = product

        @pl.when(pl.program_id(0) > 0)
        def _():
            o_ref[...] += product

    return pl.pallas_call(
        kernel,
        grid_spec=pltpu.PrefetchScalarGridSpec(
            num_scalar_prefetch=1,
            grid=(steps,),
            in_specs=[
                pl.BlockSpec(
                    (1, rows, depth), lambda i, first_ref: ((first_ref[0] + i) & (count - 1), 0, 0)
                ),
                pl.BlockSpec((1, depth, columns), lambda i, first_ref: (i, 0, 0)),
            ],
            out_specs=pl.BlockSpec((rows, columns), lambda i, first_ref: (0, 0)),
        ),
        out_shape=jax.ShapeDtypeStruct((rows, columns), jnp.float32),
        compiler_params=pltpu.CompilerParams(vmem_limit_bytes=16 * 1024 * 1024),
        cost_estimate=pl.CostEstimate(
            flops=2 * steps * rows * depth * columns,
            bytes_accessed=2 * steps * depth * (rows + columns) + 4 * rows * columns,
            transcendentals=0,
        ),
    )(first[None], weights, hidden)


def per_device(patches, norm_gain, w_in, q_gain, k_gain, mlp_bias, w_out, out_bias):
    images, seq_len, local_width = patches.shape
    mine = patches[0].T
    swapped = swap_out_weights(w_out)
    zgroup = lax.all_gather(mine, "zh", axis=0, tiled=True)
    zeros = jnp.concatenate([zgroup[:local_width]] * (w_out.shape[0] // seq_len), axis=1) * 0
    w_rows = lax.all_gather(swapped + zeros, DP, axis=0, tiled=True)
    w_rows = w_rows.reshape(NY, NZ * local_width, -1)
    guess = jnp.mean(zgroup.astype(jnp.float32), axis=0, keepdims=True)
    whole = gather_in_order(zgroup).reshape(-1, seq_len).astype(jnp.float32)
    offset = whole - guess
    first = jnp.mean(offset, axis=0, keepdims=True)
    second = jnp.mean(offset * offset, axis=0, keepdims=True)
    scale = lax.rsqrt(jnp.maximum(second - first * first, 0.0) + EPS)
    normed = ((whole - (guess + first)) * scale * norm_gain[:, None]).astype(jnp.bfloat16)
    project = lax.dot_general(
        w_in, normed, (((0,), (0,)), ((), ())), preferred_element_type=jnp.float32
    )
    head = q_gain.shape[1]
    queries = normalize(project[:head], 0) * q_gain[0][:, None]
    keys = normalize(project[head : 2 * head], 0) * k_gain[0][:, None]
    values = project[2 * head : 3 * head].astype(jnp.bfloat16)
    scores = lax.dot_general(queries, keys, (((0,), (0,)), ((), ()))) * (1.0 / head**0.5)
    probs = jax.nn.softmax(scores, axis=-1).astype(jnp.bfloat16)
    attended = lax.dot_general(
        values, probs, (((1,), (1,)), ((), ())), preferred_element_type=jnp.float32
    ).astype(jnp.bfloat16)
    mlp_hidden = jax.nn.gelu(project[3 * head :] + mlp_bias[:, None], approximate=False)
    hidden = jnp.concatenate([attended, mlp_hidden.astype(jnp.bfloat16)], axis=0)
    near, (above3, far_top, far_bottom, below3) = gather_y(
        hidden, w_rows[0, : hidden.shape[0], :seq_len] * 0
    )
    far = jnp.concatenate([far_top, far_bottom], axis=0)
    y = lax.axis_index("y")
    part = multiply_out(w_rows, jnp.stack(near), y + NY - 2)
    part = part + multiply_out(w_rows, jnp.stack((above3, far, below3)), y + 3)
    part = part.astype(jnp.bfloat16).reshape(NZ, local_width, seq_len)
    pieces = lax.all_to_all(part, "zh", 0, 0)
    total = jnp.sum(pieces.astype(jnp.float32), axis=0)
    result = mine.astype(jnp.float32) + total + out_bias[:, None]
    return result.astype(jnp.bfloat16).T[None]


def solution(mesh):
    fine = Mesh(mesh.devices.reshape(NX, 2, 2, 2, NY, NZ), AXES)
    in_specs = (
        P(DP, None, MP),
        P(),
        P(None, MP),
        P(MP, None),
        P(MP, None),
        P(MP),
        P(MP, DP),
        P(MP),
    )
    return jax.shard_map(
        per_device, mesh=fine, in_specs=in_specs, out_specs=P(DP, None, MP), check_vma=False
    )
```

```python
import jax
import jax.numpy as jnp
from jax import lax
from jax.experimental import pallas as pl
from jax.experimental.pallas import tpu as pltpu
from jax.sharding import Mesh
from jax.sharding import PartitionSpec as P

EPS = 1e-06
NX = 4
NY = 8
NZ = 4
AXES = ("x", "zlh", "zll", "c", "y", "zh")
DP = ("x", "zlh", "zll", "c")
MP = ("y", "zh")


def normalize(values, axis):
    center = values - jnp.mean(values, axis=axis, keepdims=True)
    spread = jnp.mean(center * center, axis=axis, keepdims=True)
    return center * lax.rsqrt(spread + EPS)


def shift(value, axis, count, by):
    return lax.ppermute(value, axis, [(i, (i + by) % count) for i in range(count)])


def gather_y(block, zero=None):
    half = block.shape[0] // 2
    below2, above2 = shift(block, "y", NY, 2), shift(block, "y", NY, -2)
    below1, above1 = shift(block, "y", NY, 1), shift(block, "y", NY, -1)
    late = above2 if zero is None else above2 + zero
    below3, above3 = shift(below2, "y", NY, 1), shift(late, "y", NY, -1)
    far_top = shift(below2[:half], "y", NY, 2)
    far_bottom = shift(above2[half:], "y", NY, -2)
    return (below2, below1, block, above1, above2), (above3, far_top, far_bottom, below3)


def gather_in_order(block):
    y = lax.axis_index("y")
    half = block.shape[0] // 2
    whole = jnp.zeros((NY,) + block.shape, block.dtype)
    put = lambda whole, part, index, row: lax.dynamic_update_slice(
        whole, part[None], (index & (NY - 1), row, 0)
    )
    whole = put(whole, block, y, 0)
    up = down = block
    for step in range(1, 4):
        up, down = shift(up, "y", NY, 1), shift(down, "y", NY, -1)
        whole = put(whole, up, y - step + NY, 0)
        whole = put(whole, down, y + step, 0)
    up, down = shift(up[:half], "y", NY, 1), shift(down[half:], "y", NY, -1)
    whole = put(whole, up, y + 4, 0)
    return put(whole, down, y + 4, half)


def swap_out_weights(w_out):
    pairs = [
        ((out * 4 + low) * NY + y, (y * 4 + low) * NY + out)
        for out in range(NY)
        for low in range(4)
        for y in range(NY)
    ]
    return lax.ppermute(w_out.T, ("x", "zlh", "zll", "c", "y"), pairs)


def multiply_out(weights, hidden, first):
    count, rows, depth = weights.shape
    steps, _, columns = hidden.shape

    def kernel(first_ref, w_ref, h_ref, o_ref):
        product = jnp.dot(w_ref[0], h_ref[0], preferred_element_type=jnp.float32)

        @pl.when(pl.program_id(0) == 0)
        def _():
            o_ref[...] = product

        @pl.when(pl.program_id(0) > 0)
        def _():
            o_ref[...] += product

    return pl.pallas_call(
        kernel,
        grid_spec=pltpu.PrefetchScalarGridSpec(
            num_scalar_prefetch=1,
            grid=(steps,),
            in_specs=[
                pl.BlockSpec(
                    (1, rows, depth), lambda i, first_ref: ((first_ref[0] + i) & (count - 1), 0, 0)
                ),
                pl.BlockSpec((1, depth, columns), lambda i, first_ref: (i, 0, 0)),
            ],
            out_specs=pl.BlockSpec((rows, columns), lambda i, first_ref: (0, 0)),
        ),
        out_shape=jax.ShapeDtypeStruct((rows, columns), jnp.float32),
        compiler_params=pltpu.CompilerParams(vmem_limit_bytes=16 * 1024 * 1024),
        cost_estimate=pl.CostEstimate(
            flops=2 * steps * rows * depth * columns,
            bytes_accessed=2 * steps * depth * (rows + columns) + 4 * rows * columns,
            transcendentals=0,
        ),
    )(first[None], weights, hidden)


def per_device(patches, norm_gain, w_in, q_gain, k_gain, mlp_bias, w_out, out_bias):
    images, seq_len, local_width = patches.shape
    mine = patches[0].T
    swapped = swap_out_weights(w_out)
    zgroup = lax.all_gather(mine, "zh", axis=0, tiled=True)
    zeros = jnp.concatenate([zgroup[:local_width]] * (w_out.shape[0] // seq_len), axis=1) * 0
    w_rows = lax.all_gather(swapped + zeros, DP, axis=0, tiled=True)
    w_rows = w_rows.reshape(NY, NZ * local_width, -1)
    whole = gather_in_order(zgroup).reshape(-1, seq_len)
    normed = (normalize(whole.astype(jnp.float32), 0) * norm_gain[:, None]).astype(jnp.bfloat16)
    project = lax.dot_general(
        w_in, normed, (((0,), (0,)), ((), ())), preferred_element_type=jnp.float32
    )
    head = q_gain.shape[1]
    queries = normalize(project[:head], 0) * q_gain[0][:, None]
    keys = normalize(project[head : 2 * head], 0) * k_gain[0][:, None]
    values = project[2 * head : 3 * head].astype(jnp.bfloat16)
    scores = lax.dot_general(queries, keys, (((0,), (0,)), ((), ()))) * (1.0 / head**0.5)
    probs = jax.nn.softmax(scores, axis=-1).astype(jnp.bfloat16)
    attended = lax.dot_general(
        values, probs, (((1,), (1,)), ((), ())), preferred_element_type=jnp.float32
    ).astype(jnp.bfloat16)
    mlp_hidden = jax.nn.gelu(project[3 * head :] + mlp_bias[:, None], approximate=False)
    hidden = jnp.concatenate([attended, mlp_hidden.astype(jnp.bfloat16)], axis=0)
    near, (above3, far_top, far_bottom, below3) = gather_y(
        hidden, w_rows[0, : hidden.shape[0], :seq_len] * 0
    )
    far = jnp.concatenate([far_top, far_bottom], axis=0)
    y = lax.axis_index("y")
    part = multiply_out(w_rows, jnp.stack(near), y + NY - 2)
    part = part + multiply_out(w_rows, jnp.stack((above3, far, below3)), y + 3)
    part = part.astype(jnp.bfloat16).reshape(NZ, local_width, seq_len)
    pieces = lax.all_to_all(part, "zh", 0, 0)
    total = jnp.sum(pieces.astype(jnp.float32), axis=0)
    result = mine.astype(jnp.float32) + total + out_bias[:, None]
    return result.astype(jnp.bfloat16).T[None]


def solution(mesh):
    fine = Mesh(mesh.devices.reshape(NX, 2, 2, 2, NY, NZ), AXES)
    in_specs = (
        P(DP, None, MP),
        P(),
        P(None, MP),
        P(MP, None),
        P(MP, None),
        P(MP),
        P(MP, DP),
        P(MP),
    )
    return jax.shard_map(
        per_device, mesh=fine, in_specs=in_specs, out_specs=P(DP, None, MP), check_vma=False
    )
```

```python
import jax
import jax.numpy as jnp
from jax import lax
from jax.experimental import pallas as pl
from jax.experimental.pallas import tpu as pltpu
from jax.sharding import Mesh
from jax.sharding import PartitionSpec as P

EPS = 1e-06
NX = 4
NY = 8
NZ = 4
AXES = ("x", "zlh", "zll", "c", "y", "zh")
DP = ("x", "zlh", "zll", "c")
MP = ("y", "zh")


def normalize(values, axis):
    center = values - jnp.mean(values, axis=axis, keepdims=True)
    spread = jnp.mean(center * center, axis=axis, keepdims=True)
    return center * lax.rsqrt(spread + EPS)


def shift(value, axis, count, by):
    return lax.ppermute(value, axis, [(i, (i + by) % count) for i in range(count)])


def gather_y(block, zero=None):
    half = block.shape[0] // 2
    below2, above2 = shift(block, "y", NY, 2), shift(block, "y", NY, -2)
    below1, above1 = shift(block, "y", NY, 1), shift(block, "y", NY, -1)
    below3, above3 = shift(below2, "y", NY, 1), shift(above2, "y", NY, -1)
    far_top = shift(below2[:half], "y", NY, 2)
    late = above2[half:] if zero is None else above2[half:] + zero[half:]
    far_bottom = shift(late, "y", NY, -2)
    return (below2, below1, block, above1, above2), (above3, far_top, far_bottom, below3)


def gather_in_order(block):
    y = lax.axis_index("y")
    half = block.shape[0] // 2
    whole = jnp.zeros((NY,) + block.shape, block.dtype)
    put = lambda whole, part, index, row: lax.dynamic_update_slice(
        whole, part[None], (index & (NY - 1), row, 0)
    )
    whole = put(whole, block, y, 0)
    up = down = block
    for step in range(1, 4):
        up, down = shift(up, "y", NY, 1), shift(down, "y", NY, -1)
        whole = put(whole, up, y - step + NY, 0)
        whole = put(whole, down, y + step, 0)
    up, down = shift(up[:half], "y", NY, 1), shift(down[half:], "y", NY, -1)
    whole = put(whole, up, y + 4, 0)
    return put(whole, down, y + 4, half)


def swap_out_weights(w_out):
    pairs = [
        ((out * 4 + low) * NY + y, (y * 4 + low) * NY + out)
        for out in range(NY)
        for low in range(4)
        for y in range(NY)
    ]
    return lax.ppermute(w_out.T, ("x", "zlh", "zll", "c", "y"), pairs)


def multiply_out(weights, hidden, first):
    count, rows, depth = weights.shape
    steps, _, columns = hidden.shape

    def kernel(first_ref, w_ref, h_ref, o_ref):
        product = jnp.dot(w_ref[0], h_ref[0], preferred_element_type=jnp.float32)

        @pl.when(pl.program_id(0) == 0)
        def _():
            o_ref[...] = product

        @pl.when(pl.program_id(0) > 0)
        def _():
            o_ref[...] += product

    return pl.pallas_call(
        kernel,
        grid_spec=pltpu.PrefetchScalarGridSpec(
            num_scalar_prefetch=1,
            grid=(steps,),
            in_specs=[
                pl.BlockSpec(
                    (1, rows, depth), lambda i, first_ref: ((first_ref[0] + i) & (count - 1), 0, 0)
                ),
                pl.BlockSpec((1, depth, columns), lambda i, first_ref: (i, 0, 0)),
            ],
            out_specs=pl.BlockSpec((rows, columns), lambda i, first_ref: (0, 0)),
        ),
        out_shape=jax.ShapeDtypeStruct((rows, columns), jnp.float32),
        compiler_params=pltpu.CompilerParams(vmem_limit_bytes=16 * 1024 * 1024),
        cost_estimate=pl.CostEstimate(
            flops=2 * steps * rows * depth * columns,
            bytes_accessed=2 * steps * depth * (rows + columns) + 4 * rows * columns,
            transcendentals=0,
        ),
    )(first[None], weights, hidden)


def per_device(patches, norm_gain, w_in, q_gain, k_gain, mlp_bias, w_out, out_bias):
    images, seq_len, local_width = patches.shape
    mine = patches[0].T
    swapped = swap_out_weights(w_out)
    zgroup = lax.all_gather(mine, "zh", axis=0, tiled=True)
    zeros = jnp.concatenate([zgroup[:local_width]] * (w_out.shape[0] // seq_len), axis=1) * 0
    w_rows = lax.all_gather(swapped + zeros, DP, axis=0, tiled=True)
    w_rows = w_rows.reshape(NY, NZ * local_width, -1)
    whole = gather_in_order(zgroup).reshape(-1, seq_len)
    normed = (normalize(whole.astype(jnp.float32), 0) * norm_gain[:, None]).astype(jnp.bfloat16)
    project = lax.dot_general(
        w_in, normed, (((0,), (0,)), ((), ())), preferred_element_type=jnp.float32
    )
    head = q_gain.shape[1]
    queries = normalize(project[:head], 0) * q_gain[0][:, None]
    keys = normalize(project[head : 2 * head], 0) * k_gain[0][:, None]
    values = project[2 * head : 3 * head].astype(jnp.bfloat16)
    scores = lax.dot_general(queries, keys, (((0,), (0,)), ((), ()))) * (1.0 / head**0.5)
    probs = jax.nn.softmax(scores, axis=-1).astype(jnp.bfloat16)
    attended = lax.dot_general(
        values, probs, (((1,), (1,)), ((), ())), preferred_element_type=jnp.float32
    ).astype(jnp.bfloat16)
    mlp_hidden = jax.nn.gelu(project[3 * head :] + mlp_bias[:, None], approximate=False)
    hidden = jnp.concatenate([attended, mlp_hidden.astype(jnp.bfloat16)], axis=0)
    near, (above3, far_top, far_bottom, below3) = gather_y(
        hidden, w_rows[0, : hidden.shape[0], :seq_len] * 0
    )
    far = jnp.concatenate([far_top, far_bottom], axis=0)
    y = lax.axis_index("y")
    part = multiply_out(w_rows, jnp.stack(near), y + NY - 2)
    part = part + multiply_out(w_rows, jnp.stack((above3, far, below3)), y + 3)
    part = part.astype(jnp.bfloat16).reshape(NZ, local_width, seq_len)
    pieces = lax.all_to_all(part, "zh", 0, 0)
    total = jnp.sum(pieces.astype(jnp.float32), axis=0)
    result = mine.astype(jnp.float32) + total + out_bias[:, None]
    return result.astype(jnp.bfloat16).T[None]


def solution(mesh):
    fine = Mesh(mesh.devices.reshape(NX, 2, 2, 2, NY, NZ), AXES)
    in_specs = (
        P(DP, None, MP),
        P(),
        P(None, MP),
        P(MP, None),
        P(MP, None),
        P(MP),
        P(MP, DP),
        P(MP),
    )
    return jax.shard_map(
        per_device, mesh=fine, in_specs=in_specs, out_specs=P(DP, None, MP), check_vma=False
    )
```
